32 devices in a mesh: group: 2 (over x), blk: 16 (over z, y, core).
Axes of the slice: x: 2, y: 2, z: 4, core: 2. Of those that a mesh axis runs over, the one named last changes fastest.
Arguments:
- coarse: float32 [3, 16384, 256], P(None, ('group', 'blk')), parts along dimension 1, may hold values from -6 to 6
- fine_old: float32 [192, 3, 32, 256], P(('group', 'blk')), parts along dimension 0, may hold values from -6 to 6
- refine_flags: int32 [1024], P('group'), parts along dimension 0, may hold values from 0 to 1, as said below
- new_slot: int32 [64], P('group'), parts along dimension 0, may hold values from 0 to 31, each once
- courant: float32 [512], P('group'), parts along dimension 0, may hold values from 0.05 to 0.9
Outputs:
- coarse_out: float32 [3, 16384, 256], P(None, ('group', 'blk')), parts along dimension 1
- fine_out: float32 [64, 3, 32, 256], P(('group', 'blk')), parts along dimension 0
The draws below stay inside these ranges and needn't reach their ends.
There are 2 independent parts, one for each index of `group`. The reference program is written for one: setup_inputs(seed, part) draws one part's arguments, and reference() takes and returns one part's arrays. A program takes and returns all parts, laid end to end along the dimension named above; each array names one. Nothing has to cross between parts.
Inputs may be any that keep to these rules, and one draw needn't show every extreme that they name: `refine_flags`: no two flagged blocks are adjacent; the first and last block of each owner's aligned run of 32 blocks is never flagged; each run holds at most 6 flags, some run exactly 6; 32 flags in all. `new_slot`: each slot once.
All inputs are finite; a program needn't handle non-finite values.
Results may differ from the reference program's by a relative error of at most 0.00002.
Values sent between devices are 32-bit elements; how exact they have to be, the bound alone decides.
A program may use at most 64 MiB of HBM per device.

```python
import math
import jax
import jax.numpy as jnp

COLS = 256
B_DEV = 32
CB = 16
FCAP = 6
FB = 32
NBLK = 512
NX = 8192
NFINE = 32
N_BLK = 16


def draw_refine_flags(key, part):
    key = jax.random.fold_in(key, 11)
    owner_total = NBLK // B_DEV
    patterns = jnp.array([[6, 0, 1, 1], [6, 2, 0, 0], [4, 2, 1, 1], [3, 3, 1, 1]], jnp.int32)
    first_key, second_key, third_key = jax.random.split(key, 3)
    variant = jax.random.randint(first_key, (owner_total // 4,), 0, 4)
    variant = variant.at[0].set(0)
    counts_listed = patterns[variant].reshape(-1)
    owner_order = jax.random.permutation(second_key, owner_total)
    counts = counts_listed[owner_order]
    spread = B_DEV - 2 - FCAP + 1
    owner_keys = jax.random.split(third_key, owner_total)
    shuffles = jax.vmap(lambda one_key: jax.random.permutation(one_key, spread))(owner_keys)
    placed = jnp.argsort(shuffles, axis=1, stable=True)
    chosen = (placed < counts[:, None]).astype(jnp.int32)
    before = jnp.cumsum(chosen, axis=1) - chosen
    position = jnp.arange(spread, dtype=jnp.int32)[None, :] + before + 1
    hits = (position[:, :, None] == jnp.arange(B_DEV, dtype=jnp.int32)[None, None, :]).astype(jnp.int32)
    flag_rows = jnp.sum(hits * chosen[:, :, None], axis=1)
    return flag_rows.reshape(-1).astype(jnp.int32)


def shard_levels(own_key, extent, pieces, low, top_value):
    level = 1.0
    for axis_at, shards_of in pieces:
        draws = jax.random.uniform(jax.random.fold_in(jax.random.fold_in(own_key, 6), axis_at), (shards_of,), jnp.float32, low / len(pieces), top_value / len(pieces))
        level = level * jnp.repeat(jnp.exp(draws), extent[axis_at] // shards_of).reshape((-1,) + (1,) * (len(extent) - 1 - axis_at))
    return level


def normal_values(key, dims, deviation, limit, pieces=(), kind=jnp.bfloat16):
    result = deviation * jax.random.normal(key, dims, jnp.float32)
    if pieces:
        result = result * shard_levels(key, dims, pieces, -0.22, 0.18)
    return jnp.clip(result, -limit, limit).astype(kind)


def setup_inputs(seed: int = 0, part: int = 0) -> dict:
    arg_keys = jax.random.split(jax.random.key(seed), 6)
    part_splits = jax.random.split(jax.random.fold_in(arg_keys[5], part), 6)
    return {
        "coarse": normal_values(part_splits[0], (3, NX, COLS), 1.0, 6.0, ((1, 16),), jnp.float32),
        "fine_old": normal_values(part_splits[1], (N_BLK * FCAP, 3, FB, COLS), 1.0, 6.0, ((0, 16),), jnp.float32),
        "refine_flags": draw_refine_flags(jax.random.fold_in(jax.random.fold_in(arg_keys[5], part), 71), part),
        "new_slot": jax.random.permutation(part_splits[3], NFINE).astype(jnp.int32),
        "courant": jnp.clip(jnp.exp(jax.random.uniform(part_splits[4], (COLS,), jnp.float32, math.log(0.05), math.log(0.9))), 0.05, 0.9),
    }


sound_number = 0.6


def acoustic(pressure, velocity, rim_width):
    press_flux = sound_number * 0.5 * (pressure[:-1] + pressure[1:])
    velocity_new = velocity[1:-1] - (press_flux[1:] - press_flux[:-1])
    speed_flux = sound_number * 0.5 * (velocity_new[:-1] + velocity_new[1:])
    pressure_new = pressure[2:-2] - (speed_flux[1:] - speed_flux[:-1])
    cell_count = pressure.shape[0] - 2 * rim_width
    return (pressure_new, velocity_new[1:-1],
            speed_flux[rim_width - 2:rim_width - 1 + cell_count],
            press_flux[rim_width - 1:rim_width + cell_count])


def transport(warmth, courant):
    heat_flux = courant * 0.5 * (warmth[:-1] + warmth[1:]) - 0.5 * courant * courant * (warmth[1:] - warmth[:-1])
    return warmth[1:-1] - (heat_flux[1:] - heat_flux[:-1]), heat_flux


def fine_steps(block, ghosts, courant):
    pressure, velocity, warmth = block[0], block[1], block[2]
    nothing = jnp.zeros((block.shape[2],), jnp.float32)
    flux_left = [nothing, nothing, nothing]
    flux_right = [nothing, nothing, nothing]
    for fine_round in range(2):
        fraction = 0.5 * fine_round
        edge_values = ghosts[0:2] + fraction * (ghosts[2:4] - ghosts[0:2])
        left_edge, right_edge = edge_values[0], edge_values[1]
        for substep in range(4):
            padded = jnp.concatenate([left_edge[0][None], pressure, right_edge[0][None]], 0)
            press_flux = sound_number * 0.5 * (padded[:-1] + padded[1:])
            velocity = velocity - (press_flux[1:] - press_flux[:-1])
            padded = jnp.concatenate([left_edge[1][None], velocity, right_edge[1][None]], 0)
            speed_flux = sound_number * 0.5 * (padded[:-1] + padded[1:])
            pressure = pressure - (speed_flux[1:] - speed_flux[:-1])
            flux_left = [flux_left[0] + speed_flux[0], flux_left[1] + press_flux[0], flux_left[2]]
            flux_right = [flux_right[0] + speed_flux[-1], flux_right[1] + press_flux[-1], flux_right[2]]
        padded = jnp.concatenate([left_edge[2][None], warmth, right_edge[2][None]], 0)
        warmth, heat_flux = transport(padded, courant)
        flux_left = [flux_left[0], flux_left[1], flux_left[2] + heat_flux[0]]
        flux_right = [flux_right[0], flux_right[1], flux_right[2] + heat_flux[-1]]
    return jnp.stack([pressure, velocity, warmth]), jnp.stack(flux_left), jnp.stack(flux_right)


def average_down(blocks):
    return 0.5 * (blocks[:, :, 0::2] + blocks[:, :, 1::2])


def apply_fine(field, face_sums, flag_row, avg_rows, reg_rows):
    block_count = flag_row.shape[0]
    columns = field.shape[2]
    blocks = field.reshape(3, block_count, CB, columns)
    refined = flag_row == 1
    left_fix = face_sums[:, :block_count] - 0.5 * reg_rows[:, 0].transpose(1, 0, 2)
    right_fix = face_sums[:, 1:] - 0.5 * reg_rows[:, 1].transpose(1, 0, 2)
    nothing = jnp.zeros_like(left_fix[:, :1])
    marked = refined[None, :, None]
    last_add = jnp.concatenate([jnp.where(marked, left_fix, 0.0)[:, 1:], nothing], 1)
    first_add = jnp.concatenate([nothing, jnp.where(marked, -right_fix, 0.0)[:, :-1]], 1)
    blocks = jnp.where(refined[None, :, None, None], avg_rows.transpose(1, 0, 2, 3), blocks)
    blocks = blocks.at[:, :, CB - 1].add(last_add).at[:, :, 0].add(first_add)
    return blocks.reshape(3, block_count * CB, columns)


def wrap_cycle(field, rim_width):
    return jnp.concatenate([field[:, -rim_width:], field, field[:, :rim_width]], 1)


def coarse_step(coarse, courant):
    padded = wrap_cycle(coarse, 2)
    pressure, velocity = padded[0], padded[1]
    warmth = padded[2][1:-1]
    press_sum = jnp.zeros((coarse.shape[1] + 1, coarse.shape[2]), jnp.float32)
    speed_sum = press_sum
    for substep in range(4):
        if substep > 0:
            pair_rim = wrap_cycle(jnp.stack([pressure, velocity]), 2)
            pressure, velocity = pair_rim[0], pair_rim[1]
        pressure, velocity, speed_flux, press_flux = acoustic(pressure, velocity, 2)
        speed_sum = speed_sum + speed_flux
        press_sum = press_sum + press_flux
    warmth, heat_flux = transport(warmth, courant)
    face_sums = jnp.stack([speed_sum[::CB], press_sum[::CB], heat_flux[::CB]])
    return jnp.stack([pressure, velocity, warmth]), face_sums


def reference(coarse, fine_old, refine_flags, new_slot, courant):
    fine_count = new_slot.shape[0]
    flag_total = jnp.cumsum(refine_flags).astype(jnp.int32)
    before = flag_total - refine_flags
    refined_id = flag_total - 1
    parents = jnp.nonzero(refine_flags, size=fine_count)[0].astype(jnp.int32)
    owners = parents // B_DEV
    slots = refined_id[parents] - before[owners * B_DEV]
    fine = fine_old[owners * FCAP + slots]
    advanced, face_sums = coarse_step(coarse, courant)
    edge_index = jnp.stack([parents * CB - 1, (parents + 1) * CB], 1)
    ghosts = jnp.concatenate([coarse[:, edge_index], advanced[:, edge_index]], 2).transpose(1, 2, 0, 3)
    fine_new, left_regs, right_regs = jax.vmap(fine_steps, (0, 0, None))(fine, ghosts, courant)
    averaged = average_down(fine_new)
    registers = jnp.stack([left_regs, right_regs], 1)
    rows = jnp.clip(refined_id, 0, fine_count - 1)
    coarse_out = apply_fine(advanced, face_sums, refine_flags, averaged[rows], registers[rows])
    fine_out = jnp.zeros_like(fine_new).at[new_slot].set(fine_new)
    return coarse_out, fine_out
```

```python
import jax
import jax.numpy as jnp
from jax import lax
from jax.sharding import PartitionSpec as P

B_DEV = 32
CB = 16
FCAP = 6
F_DEV = 2


sound_number = 0.6


def transport(warmth, courant):
    heat_flux = courant * 0.5 * (warmth[:-1] + warmth[1:]) - 0.5 * courant * courant * (
        warmth[1:] - warmth[:-1]
    )
    return (warmth[1:-1] - (heat_flux[1:] - heat_flux[:-1]), heat_flux)


def fine_steps(block, ghosts, courant):
    pressure, velocity, warmth = (block[0], block[1], block[2])
    nothing = jnp.zeros((block.shape[2],), jnp.float32)
    flux_left = [nothing, nothing, nothing]
    flux_right = [nothing, nothing, nothing]
    for fine_round in range(2):
        fraction = 0.5 * fine_round
        edge_values = ghosts[0:2] + fraction * (ghosts[2:4] - ghosts[0:2])
        left_edge, right_edge = (edge_values[0], edge_values[1])
        for substep in range(4):
            padded = jnp.concatenate([left_edge[0][None], pressure, right_edge[0][None]], 0)
            press_flux = sound_number * 0.5 * (padded[:-1] + padded[1:])
            velocity = velocity - (press_flux[1:] - press_flux[:-1])
            padded = jnp.concatenate([left_edge[1][None], velocity, right_edge[1][None]], 0)
            speed_flux = sound_number * 0.5 * (padded[:-1] + padded[1:])
            pressure = pressure - (speed_flux[1:] - speed_flux[:-1])
            flux_left = [flux_left[0] + speed_flux[0], flux_left[1] + press_flux[0], flux_left[2]]
            flux_right = [
                flux_right[0] + speed_flux[-1],
                flux_right[1] + press_flux[-1],
                flux_right[2],
            ]
        padded = jnp.concatenate([left_edge[2][None], warmth, right_edge[2][None]], 0)
        warmth, heat_flux = transport(padded, courant)
        flux_left = [flux_left[0], flux_left[1], flux_left[2] + heat_flux[0]]
        flux_right = [flux_right[0], flux_right[1], flux_right[2] + heat_flux[-1]]
    return (jnp.stack([pressure, velocity, warmth]), jnp.stack(flux_left), jnp.stack(flux_right))


def average_down(blocks):
    return 0.5 * (blocks[:, :, 0::2] + blocks[:, :, 1::2])


def apply_fine(field, face_sums, flag_row, avg_rows, reg_rows):
    block_count = flag_row.shape[0]
    columns = field.shape[2]
    blocks = field.reshape(3, block_count, CB, columns)
    refined = flag_row == 1
    left_fix = face_sums[:, :block_count] - 0.5 * reg_rows[:, 0].transpose(1, 0, 2)
    right_fix = face_sums[:, 1:] - 0.5 * reg_rows[:, 1].transpose(1, 0, 2)
    nothing = jnp.zeros_like(left_fix[:, :1])
    marked = refined[None, :, None]
    last_add = jnp.concatenate([jnp.where(marked, left_fix, 0.0)[:, 1:], nothing], 1)
    first_add = jnp.concatenate([nothing, jnp.where(marked, -right_fix, 0.0)[:, :-1]], 1)
    blocks = jnp.where(refined[None, :, None, None], avg_rows.transpose(1, 0, 2, 3), blocks)
    blocks = blocks.at[:, :, CB - 1].add(last_add).at[:, :, 0].add(first_add)
    return blocks.reshape(3, block_count * CB, columns)


def halo_rows(block, width):
    count = lax.axis_size("blk")
    forward = [(i, (i + 1) % count) for i in range(count)]
    backward = [(target, source) for source, target in forward]
    low = lax.ppermute(block[:, -width:], "blk", forward)
    high = lax.ppermute(block[:, :width], "blk", backward)
    return jnp.concatenate([low, block, high], axis=1)


def coarse_step(coarse, courant):
    rows = coarse.shape[1]
    padded = halo_rows(coarse, 8)
    pressure, velocity = padded[0], padded[1]
    speed_sum = press_sum = 0.0
    for substep in range(4):
        press_flux = sound_number * 0.5 * (pressure[:-1] + pressure[1:])
        velocity = velocity[1:-1] - (press_flux[1:] - press_flux[:-1])
        speed_flux = sound_number * 0.5 * (velocity[:-1] + velocity[1:])
        pressure = pressure[2:-2] - (speed_flux[1:] - speed_flux[:-1])
        velocity = velocity[1:-1]
        rim = 6 - 2 * substep
        speed_sum = speed_sum + speed_flux[rim : rim + rows + 1]
        press_sum = press_sum + press_flux[rim + 1 : rim + 2 + rows]
    warmth, heat_flux = transport(padded[2][7:-7], courant)
    face_sums = jnp.stack([speed_sum[::CB], press_sum[::CB], heat_flux[::CB]])
    return (jnp.stack([pressure, velocity, warmth]), face_sums)


def per_device(coarse, fine_old, refine_flags, new_slot, courant):
    rank_here = lax.axis_index("blk")
    fine_count = new_slot.shape[0]
    block_all = jnp.arange(refine_flags.shape[0], dtype=jnp.int32)
    first_id = jnp.sum(jnp.where(block_all < rank_here * B_DEV, refine_flags, 0))
    my_flags = lax.dynamic_slice_in_dim(refine_flags, rank_here * B_DEV, B_DEV)
    block_ids = jnp.arange(B_DEV, dtype=jnp.int32)
    my_rank = jnp.sum(jnp.where(block_ids[None, :] < block_ids[:, None], my_flags[None, :], 0), axis=1)
    slot_ids = jnp.arange(FCAP, dtype=jnp.int32)
    slot_hit = (my_flags[None, :] == 1) & (my_rank[None, :] == slot_ids[:, None])
    slot_live = jnp.any(slot_hit, axis=1)
    slot_block = jnp.where(
        slot_live, jnp.sum(jnp.where(slot_hit, block_ids[None, :], 0), axis=1), 1
    )
    slot_fine = jnp.clip(first_id + slot_ids, 0, fine_count - 1)
    slot_dest = jnp.where(slot_live, new_slot[slot_fine], -1)
    row_ids = jnp.arange(fine_count, dtype=jnp.int32)
    send_match = slot_dest[None, :] == row_ids[:, None]
    send_slot = jnp.sum(jnp.where(send_match, slot_ids[None, :], 0), axis=1)
    send_live = jnp.any(send_match, axis=1)
    advanced, face_sums = coarse_step(coarse, courant)
    edge_index = jnp.stack([slot_block * CB - 1, (slot_block + 1) * CB], 1)
    ghosts = jnp.concatenate([coarse[:, edge_index], advanced[:, edge_index]], 2).transpose(
        1, 2, 0, 3
    )
    fine_new, left_regs, right_regs = jax.vmap(fine_steps, (0, 0, None))(
        fine_old, ghosts, courant
    )
    packed = jnp.where(send_live[:, None, None, None], fine_new[send_slot], 0.0)
    fine_out = lax.psum_scatter(packed, "blk", scatter_dimension=0, tiled=True)
    averaged = average_down(fine_new)
    registers = jnp.stack([left_regs, right_regs], 1)
    block_rows = jnp.clip(my_rank, 0, FCAP - 1)
    coarse_out = apply_fine(
        advanced, face_sums, my_flags, averaged[block_rows], registers[block_rows]
    )
    return (coarse_out, fine_out)


def solution(mesh):
    placed = (
        P(None, ("group", "blk"), None),
        P(("group", "blk"), None, None, None),
        P("group"),
        P("group"),
        P("group"),
    )
    return jax.shard_map(
        per_device,
        mesh=mesh,
        in_specs=placed,
        out_specs=(P(None, ("group", "blk"), None), P(("group", "blk"), None, None, None)),
        check_vma=False,
    )
```

```python
import functools

import jax
import jax.numpy as jnp
from jax import lax
from jax.experimental import pallas as pl
from jax.experimental.pallas import tpu as pltpu
from jax.sharding import PartitionSpec as P

B_DEV = 32
CB = 16
FCAP = 6
FB = 32
F_DEV = 2
RIM = 8
QUAD = 4
ROWS_AT_ONCE = 64
HALF = 0.3
MESH = pl.DeviceIdType.MESH
VMEM_LIMIT = 48 * 1024 * 1024
CHUNKS = ((2, 0, 32), (0, 0, 32), (1, 0, 32))


def shifted(field):
    count = field.shape[0]
    return pltpu.roll(field, 1, 0), pltpu.roll(field, count - 1, 0)


def acoustic_substeps(pressure, velocity):
    press_sum = speed_sum = 0.0
    for substep in range(4):
        press_sum = press_sum + pressure
        below, above = shifted(pressure)
        velocity = velocity - HALF * (above - below)
        speed_sum = speed_sum + velocity
        below, above = shifted(velocity)
        pressure = pressure - HALF * (above - below)
    return pressure, velocity, press_sum, speed_sum


def heat_flux(low, high, courant):
    return 0.5 * courant * (low + high) - 0.5 * courant * courant * (high - low)


def transported(warmth, below, above, courant):
    return warmth - (heat_flux(warmth, above, courant) - heat_flux(below, warmth, courant))


def local_kernel(flags, slots, courant, coarse, fine_old, out, fine_new, table,
                 padded, fine, press_total, speed_total, pairs, where_at, sems):
    rows, columns = coarse.shape[1], coarse.shape[2]
    owners = flags.shape[0] // B_DEV
    get_coarse = pltpu.make_async_copy(coarse, padded.at[:, pl.ds(RIM, rows)], sems.at[0])
    get_coarse.start()
    get_fine = pltpu.make_async_copy(fine_old, fine, sems.at[1])
    get_fine.start()
    me = lax.axis_index("blk")

    def list_owner(owner, base):
        total = flags[owner * B_DEV]
        for at in range(1, B_DEV):
            total = total + flags[owner * B_DEV + at]

        def list_block(rank, carry):
            table[slots[base + rank]] = owner * FCAP + rank
            return carry

        lax.fori_loop(0, total, list_block, 0)
        return base + total

    lax.fori_loop(0, owners, list_owner, 0)
    count = jnp.int32(0)
    for block in range(B_DEV):
        where_at[count] = block
        count = count + flags[me * B_DEV + block]

    get_coarse.wait()
    for first in range(0, columns, 128):
        lanes = slice(first, first + 128)

        def advance(step, carry):
            start = pl.multiple_of(step * ROWS_AT_ONCE, ROWS_AT_ONCE)
            span = pl.ds(start, ROWS_AT_ONCE + 2 * RIM)
            here = pl.ds(start, ROWS_AT_ONCE)
            keep = slice(RIM, RIM + ROWS_AT_ONCE)
            results = acoustic_substeps(padded[0, span, lanes], padded[1, span, lanes])
            out[0, here, lanes] = results[0][keep]
            out[1, here, lanes] = results[1][keep]
            press_total[here, lanes] = results[2][keep]
            speed_total[here, lanes] = results[3][keep]
            warmth = padded[2, span, lanes]
            below, above = shifted(warmth)
            out[2, here, lanes] = transported(warmth, below, above, courant[:, lanes])[keep]
            return carry

        lax.fori_loop(0, rows // ROWS_AT_ONCE, advance, 0)

    get_fine.wait()
    row_at = lax.broadcasted_iota(jnp.int32, (FB, columns), 0)
    eight = lax.broadcasted_iota(jnp.int32, (RIM, columns), 0)
    number = courant[...]

    def with_edges(field, left, right):
        below, above = shifted(field)
        return (jnp.where(row_at == 0, left, below), jnp.where(row_at == FB - 1, right, above))

    def refine(slot, carry):
        begin = pl.multiple_of(where_at[slot] * CB, CB)
        before = pl.ds(begin - RIM, RIM)
        after = pl.ds(begin + CB, RIM)
        old = [(padded[f, pl.ds(begin, RIM)][RIM - 1:], padded[f, pl.ds(begin + CB + RIM, RIM)][:1])
               for f in range(3)]
        new = [(out[f, before][RIM - 1:], out[f, after][:1]) for f in range(3)]
        pressure, velocity, warmth = fine[slot, 0], fine[slot, 1], fine[slot, 2]
        regs = [[0.0, 0.0, 0.0], [0.0, 0.0, 0.0]]
        for fine_round in range(2):
            edges = [[o + 0.5 * fine_round * (n - o) for o, n in zip(old[f], new[f])] for f in range(3)]
            press_ends = [0.0, 0.0]
            speed_ends = [0.0, 0.0]
            for substep in range(4):
                press_ends = [press_ends[0] + pressure[:1], press_ends[1] + pressure[FB - 1:]]
                below, above = with_edges(pressure, *edges[0])
                velocity = velocity - HALF * (above - below)
                speed_ends = [speed_ends[0] + velocity[:1], speed_ends[1] + velocity[FB - 1:]]
                below, above = with_edges(velocity, *edges[1])
                pressure = pressure - HALF * (above - below)
            heat = [heat_flux(edges[2][0], warmth[:1], number),
                    heat_flux(warmth[FB - 1:], edges[2][1], number)]
            below, above = with_edges(warmth, *edges[2])
            warmth = transported(warmth, below, above, number)
            for side in range(2):
                regs[side][0] = regs[side][0] + HALF * (4.0 * edges[1][side] + speed_ends[side])
                regs[side][1] = regs[side][1] + HALF * (4.0 * edges[0][side] + press_ends[side])
                regs[side][2] = regs[side][2] + heat[side]
        fine_new[slot, 0] = pressure
        fine_new[slot, 1] = velocity
        fine_new[slot, 2] = warmth

        def face(total, low, high):
            return HALF * (total[pl.ds(low, RIM)][RIM - 1:] + total[pl.ds(high, RIM)][:1])

        left = [face(speed_total, begin - RIM, begin), face(press_total, begin - RIM, begin),
                heat_flux(old[2][0], padded[2, pl.ds(begin + RIM, RIM)][:1], number)]
        right = [face(speed_total, begin + RIM, begin + CB), face(press_total, begin + RIM, begin + CB),
                 heat_flux(padded[2, pl.ds(begin + CB, RIM)][RIM - 1:], old[2][1], number)]
        for f in range(3):
            out[f, before] = out[f, before] + jnp.where(eight == RIM - 1, left[f] - 0.5 * regs[0][f], 0.0)
            out[f, after] = out[f, after] - jnp.where(eight == 0, right[f] - 0.5 * regs[1][f], 0.0)
            for at in range(columns // 128):
                lanes = slice(at * 128, at * 128 + 128)
                half = pairs.at[f * (columns // 128) + at]
                half[...] = (pressure, velocity, warmth)[f][:, lanes]
                out[f, pl.ds(begin, CB), lanes] = 0.5 * (
                    half[pl.ds(0, CB, 2)] + half[pl.ds(1, CB, 2)])
        return carry

    lax.fori_loop(0, count, refine, 0)


def local_step(flags, slots, courant, coarse, fine_old):
    rows, columns = coarse.shape[1], coarse.shape[2]
    return pl.pallas_call(
        local_kernel,
        out_shape=(
            jax.ShapeDtypeStruct(coarse.shape, jnp.float32),
            jax.ShapeDtypeStruct(fine_old.shape, jnp.float32),
            jax.ShapeDtypeStruct(slots.shape, jnp.int32),
        ),
        in_specs=[
            pl.BlockSpec(memory_space=pltpu.SMEM),
            pl.BlockSpec(memory_space=pltpu.SMEM),
            pl.BlockSpec(memory_space=pltpu.VMEM),
            pl.BlockSpec(memory_space=pl.ANY),
            pl.BlockSpec(memory_space=pl.ANY),
        ],
        out_specs=(
            pl.BlockSpec(memory_space=pltpu.VMEM),
            pl.BlockSpec(memory_space=pltpu.VMEM),
            pl.BlockSpec(memory_space=pltpu.SMEM),
        ),
        scratch_shapes=[
            pltpu.VMEM((3, rows + 2 * RIM, columns), jnp.float32),
            pltpu.VMEM(fine_old.shape, jnp.float32),
            pltpu.VMEM((rows, columns), jnp.float32),
            pltpu.VMEM((rows, columns), jnp.float32),
            pltpu.VMEM((3 * (columns // 128), FB, 128), jnp.float32),
            pltpu.SMEM((B_DEV,), jnp.int32),
            pltpu.SemaphoreType.DMA((2,)),
        ],
        compiler_params=pltpu.CompilerParams(vmem_limit_bytes=VMEM_LIMIT),
        name="local_step",
    )(flags, slots, courant[None, :], coarse, fine_old)


def move_kernel(devices, table, courant, coarse, fine, moved, edges, windows, *scratch):
    parts = len(CHUNKS)
    gathered, leaving, landed = scratch[:parts], scratch[parts:2 * parts], scratch[2 * parts:3 * parts]
    core_send, core_recv, pair_send, pair_recv, pass_send, pass_recv, line_send, line_recv, rim_sems = scratch[3 * parts:]
    rows, columns = coarse.shape[1], coarse.shape[2]
    line = devices // QUAD
    group = lax.axis_index("group")
    me = lax.axis_index("blk")
    spot = lax.rem(me, QUAD)
    place = me // QUAD
    core = me + 1 - 2 * lax.rem(me, 2)
    pair = me + 2 - 4 * (spot // 2)
    up = lax.rem(me + 1, devices)
    down = lax.rem(me + devices - 1, devices)
    others = [lax.rem(me + QUAD * step, devices) for step in range(line)]

    barrier = pltpu.get_barrier_semaphore()
    greeted = [core, pair, up, down] + others[1:]
    for other in greeted:
        pl.semaphore_signal(barrier, inc=1, device_id=(group, other), device_id_type=MESH)

    inner = [
        pltpu.make_async_copy(coarse.at[:, pl.ds(0, 2 * RIM)], windows.at[0, :, pl.ds(RIM, 2 * RIM)], rim_sems.at[0]),
        pltpu.make_async_copy(coarse.at[:, pl.ds(rows - 2 * RIM, 2 * RIM)], windows.at[1, :, pl.ds(0, 2 * RIM)], rim_sems.at[1]),
    ]
    for copy in inner:
        copy.start()
    for at, (f, r, size) in enumerate(CHUNKS):
        for slot in range(FCAP):
            gathered[at][slot] = fine[slot, f, r:r + size]
    pl.semaphore_wait(barrier, len(greeted))

    def remote(source, target, send, recv, device):
        return pltpu.make_async_remote_copy(
            src_ref=source, dst_ref=target, send_sem=send, recv_sem=recv,
            device_id=(group, device), device_id_type=MESH)

    own, from_core, from_pair, from_far = [pl.ds(FCAP * at, FCAP) for at in range(QUAD)]
    to_pair, to_core, passed, along = [], [], [], []
    for at in range(parts):
        buffer = gathered[at]
        to_pair.append(remote(buffer.at[own], buffer.at[from_pair], pair_send.at[at], pair_recv.at[at], pair))
        to_core.append(remote(buffer.at[own], buffer.at[from_core], core_send.at[at], core_recv.at[at], core))
        passed.append(remote(buffer.at[from_pair], buffer.at[from_far], pass_send.at[at], pass_recv.at[at], core))
        along.append([
            remote(leaving[at].at[step - 1], landed[at].at[step],
                   line_send.at[at * line + step], line_recv.at[at * line + step], others[step])
            for step in range(1, line)])
        to_pair[at].start()
        to_core[at].start()
    rims = [
        remote(coarse.at[:, pl.ds(0, RIM)], windows.at[1, :, pl.ds(2 * RIM, RIM)], rim_sems.at[2], rim_sems.at[3], down),
        remote(coarse.at[:, pl.ds(rows - RIM, RIM)], windows.at[0, :, pl.ds(0, RIM)], rim_sems.at[4], rim_sems.at[5], up),
    ]
    for copy in rims:
        copy.start()

    def held_at(code):
        owner = code // FCAP
        theirs = lax.rem(owner, QUAD)
        low = (theirs + spot) % 2
        high = (theirs // 2 + spot // 2) % 2
        return (2 * high + low) * FCAP + code - owner * FCAP

    def send_along(at):
        for step in list(range(1, line)) + [0]:
            for t in range(F_DEV):
                value = gathered[at][held_at(table[others[step] * F_DEV + t])]
                if step:
                    leaving[at][step - 1, t] = value
                else:
                    landed[at][0, t] = value
            if step:
                along[at][step - 1].start()

    for at in range(parts + 1):
        if at < parts:
            to_pair[at].wait_recv()
            passed[at].start()
        if at >= 1:
            to_core[at - 1].wait_recv()
            passed[at - 1].wait_recv()
            send_along(at - 1)
        if at == 0:
            for copy in inner + rims:
                copy.wait()
            for side in range(2):
                keep = slice(RIM, 2 * RIM)
                put = slice(side * RIM, (side + 1) * RIM)
                results = acoustic_substeps(windows[side, 0], windows[side, 1])
                edges[0, put] = results[0][keep]
                edges[1, put] = results[1][keep]
                warmth = windows[side, 2]
                below, above = shifted(warmth)
                edges[2, put] = transported(warmth, below, above, courant[...])[keep]

    for at, (f, r, size) in enumerate(CHUNKS):
        for copy in along[at]:
            copy.wait_recv()
        for t in range(F_DEV):
            origin = table[me * F_DEV + t] // (FCAP * QUAD)
            step = (place - origin + line) % line
            moved[t, f, r:r + size] = landed[at][step, t]
    for at in range(parts):
        for copy in [to_pair[at], to_core[at], passed[at]] + along[at]:
            copy.wait_send()


def move(devices, table, courant, coarse, fine):
    columns = coarse.shape[2]
    line = devices // QUAD
    parts = len(CHUNKS)

    def per_chunk(*lead):
        return [pltpu.VMEM((*lead, size, columns), jnp.float32) for f, r, size in CHUNKS]

    dma = pltpu.SemaphoreType.DMA
    return pl.pallas_call(
        functools.partial(move_kernel, devices),
        out_shape=(
            jax.ShapeDtypeStruct((F_DEV, 3, FB, columns), jnp.float32),
            jax.ShapeDtypeStruct((3, 2 * RIM, columns), jnp.float32),
        ),
        in_specs=[
            pl.BlockSpec(memory_space=pltpu.SMEM),
            pl.BlockSpec(memory_space=pltpu.VMEM),
            pl.BlockSpec(memory_space=pl.ANY),
            pl.BlockSpec(memory_space=pltpu.VMEM),
        ],
        out_specs=(
            pl.BlockSpec(memory_space=pltpu.VMEM),
            pl.BlockSpec(memory_space=pltpu.VMEM),
        ),
        scratch_shapes=[
            pltpu.VMEM((2, 3, 3 * RIM, columns), jnp.float32),
            *per_chunk(QUAD * FCAP),
            *per_chunk(line - 1, F_DEV),
            *per_chunk(line, F_DEV),
            dma((parts,)), dma((parts,)), dma((parts,)), dma((parts,)), dma((parts,)), dma((parts,)),
            dma((parts * line,)), dma((parts * line,)), dma((6,)),
        ],
        compiler_params=pltpu.CompilerParams(
            collective_id=0, has_side_effects=True, vmem_limit_bytes=VMEM_LIMIT),
        name="move",
    )(table, courant[None, :], coarse, fine)


def per_device(devices, coarse, fine_old, refine_flags, new_slot, courant):
    coarse_out, fine_new, table = local_step(refine_flags, new_slot, courant, coarse, fine_old)
    fine_out, edges = move(devices, table, courant, coarse, fine_new)
    coarse_out = lax.dynamic_update_slice(coarse_out, edges[:, :RIM], (0, 0, 0))
    coarse_out = lax.dynamic_update_slice(
        coarse_out, edges[:, RIM:], (0, coarse.shape[1] - RIM, 0))
    return coarse_out, fine_out


def solution(mesh):
    placed = (
        P(None, ("group", "blk"), None),
        P(("group", "blk"), None, None, None),
        P("group"),
        P("group"),
        P("group"),
    )
    return jax.shard_map(
        functools.partial(per_device, mesh.shape["blk"]),
        mesh=mesh,
        in_specs=placed,
        out_specs=(P(None, ("group", "blk"), None), P(("group", "blk"), None, None, None)),
        check_vma=False,
    )
```

```python
import functools

import jax
import jax.numpy as jnp
from jax import lax
from jax.experimental import pallas as pl
from jax.experimental.pallas import tpu as pltpu
from jax.sharding import PartitionSpec as P

B_DEV = 32
CB = 16
FCAP = 6
FB = 32
F_DEV = 2
RIM = 8
QUAD = 4
ROWS_AT_ONCE = 64
PARENTS = 8
HALF = 0.3
MESH = pl.DeviceIdType.MESH
VMEM_LIMIT = 48 * 1024 * 1024
CHUNKS = ((2, 0, 16), (2, 16, 16), (0, 0, 16), (0, 16, 16), (1, 0, 16), (1, 16, 16))


def shifted(field):
    count = field.shape[0]
    return pltpu.roll(field, 1, 0), pltpu.roll(field, count - 1, 0)


def acoustic_substeps(pressure, velocity):
    press_sum = speed_sum = 0.0
    for substep in range(4):
        press_sum = press_sum + pressure
        below, above = shifted(pressure)
        velocity = velocity - HALF * (above - below)
        speed_sum = speed_sum + velocity
        below, above = shifted(velocity)
        pressure = pressure - HALF * (above - below)
    return pressure, velocity, press_sum, speed_sum


def heat_flux(low, high, courant):
    return 0.5 * courant * (low + high) - 0.5 * courant * courant * (high - low)


def transported(warmth, below, above, courant):
    return warmth - (heat_flux(warmth, above, courant) - heat_flux(below, warmth, courant))


def plan_kernel(flags_at, slots_at, plan, flags, slots, sems):
    get_flags = pltpu.make_async_copy(flags_at, flags, sems.at[0])
    get_slots = pltpu.make_async_copy(slots_at, slots, sems.at[1])
    get_flags.start()
    get_slots.start()
    get_flags.wait()
    get_slots.wait()
    me = lax.axis_index("blk")
    owners = flags.shape[0] // B_DEV
    fine_count = slots.shape[0]

    def list_owner(owner, base):
        total = flags[owner * B_DEV]
        for at in range(1, B_DEV):
            total = total + flags[owner * B_DEV + at]

        def list_block(rank, carry):
            plan[slots[base + rank]] = owner * FCAP + rank
            return carry

        lax.fori_loop(0, total, list_block, 0)
        return base + total

    lax.fori_loop(0, owners, list_owner, 0)
    for slot in range(PARENTS):
        plan[fine_count + slot] = 0
    ranks = fine_count + PARENTS + 1
    plan[ranks - 1] = FCAP
    plan[ranks + B_DEV] = FCAP
    count = jnp.int32(0)
    for block in range(1, B_DEV - 1):
        flag = flags[me * B_DEV + block]
        before = plan[fine_count + count]
        plan[fine_count + count] = jnp.where(flag == 1, block - 1, before)
        plan[ranks + block] = jnp.where(flag == 1, count, FCAP)
        count = count + flag
    plan[ranks] = FCAP
    plan[ranks + B_DEV - 1] = FCAP


def make_plan(flags, slots):
    return pl.pallas_call(
        plan_kernel,
        out_shape=jax.ShapeDtypeStruct((slots.shape[0] + PARENTS + B_DEV + 2,), jnp.int32),
        in_specs=[pl.BlockSpec(memory_space=pltpu.HBM)] * 2,
        out_specs=pl.BlockSpec(memory_space=pltpu.SMEM),
        scratch_shapes=[
            pltpu.SMEM(flags.shape, jnp.int32),
            pltpu.SMEM(slots.shape, jnp.int32),
            pltpu.SemaphoreType.DMA((2,)),
        ],
        name="make_plan",
    )(flags, slots)


def step_kernel(devices, plan, courant, coarse, fine, out, moved,
                windows, blocks, averages, fixes, halves, *scratch):
    parts = len(CHUNKS)
    gathered, leaving, landed = scratch[:parts], scratch[parts:2 * parts], scratch[2 * parts:3 * parts]
    core_send, core_recv, pair_send, pair_recv, pass_send, pass_recv, line_send, line_recv, rim_sems = scratch[3 * parts:]
    rows, columns = coarse.shape[1], coarse.shape[2]
    fine_count = devices * F_DEV
    line = devices // QUAD
    group = lax.axis_index("group")
    me = lax.axis_index("blk")
    spot = lax.rem(me, QUAD)
    place = me // QUAD
    core = me + 1 - 2 * lax.rem(me, 2)
    pair = me + 2 - 4 * (spot // 2)
    up = lax.rem(me + 1, devices)
    down = lax.rem(me + devices - 1, devices)
    others = [lax.rem(me + QUAD * step, devices) for step in range(line)]

    barrier = pltpu.get_barrier_semaphore()
    greeted = [core, pair, up, down] + others[1:]
    for other in greeted:
        pl.semaphore_signal(barrier, inc=1, device_id=(group, other), device_id_type=MESH)

    averages[FCAP] = jnp.zeros(averages.shape[1:], jnp.float32)
    fixes[FCAP] = jnp.zeros(fixes.shape[1:], jnp.float32)

    def copy_block(block, carry):
        for f in range(3):
            blocks[block, f] = coarse[f, pl.ds(pl.multiple_of(block * CB, CB), CB)]
        return carry

    lax.fori_loop(0, B_DEV, copy_block, 0)

    def remote(source, target, send, recv, device):
        return pltpu.make_async_remote_copy(
            src_ref=source, dst_ref=target, send_sem=send, recv_sem=recv,
            device_id=(group, device), device_id_type=MESH)

    own, from_core, from_pair, from_far = [pl.ds(FCAP * at, FCAP) for at in range(QUAD)]
    to_pair, to_core, passed, along = [], [], [], []
    for at in range(parts):
        buffer = gathered[at]
        to_pair.append(remote(buffer.at[own], buffer.at[from_pair], pair_send.at[at], pair_recv.at[at], pair))
        to_core.append(remote(buffer.at[own], buffer.at[from_core], core_send.at[at], core_recv.at[at], core))
        passed.append(remote(buffer.at[from_pair], buffer.at[from_far], pass_send.at[at], pass_recv.at[at], core))
        along.append([
            remote(leaving[at].at[step - 1], landed[at].at[step],
                   line_send.at[at * line + step], line_recv.at[at * line + step], others[step])
            for step in range(1, line)])
    rims = [
        remote(coarse.at[:, pl.ds(0, RIM)], windows.at[1, :, pl.ds(2 * RIM, RIM)], rim_sems.at[0], rim_sems.at[1], down),
        remote(coarse.at[:, pl.ds(rows - RIM, RIM)], windows.at[0, :, pl.ds(0, RIM)], rim_sems.at[2], rim_sems.at[3], up),
    ]

    number = courant[...]
    row_at = lax.broadcasted_iota(jnp.int32, (FB, columns), 0)
    eight = lax.broadcasted_iota(jnp.int32, (RIM, columns), 0)

    def with_edges(field, left, right):
        below, above = shifted(field)
        return (jnp.where(row_at == 0, left, below), jnp.where(row_at == FB - 1, right, above))

    def around(slot, f):
        block = plan[fine_count + slot]
        return jnp.concatenate([blocks[block, f], blocks[block + 1, f], blocks[block + 2, f]], 0)

    def ghosts(old, new):
        pairs = [(old[CB - 1:CB], new[CB - 1:CB]), (old[2 * CB:2 * CB + 1], new[2 * CB:2 * CB + 1])]
        return [[o + 0.5 * fine_round * (n - o) for o, n in pairs] for fine_round in range(2)]

    def face(total):
        return [HALF * (total[CB - 1:CB] + total[CB:CB + 1]),
                HALF * (total[2 * CB - 1:2 * CB] + total[2 * CB:2 * CB + 1])]

    def keep_block(slot, f, value, faces, regs):
        for at, (field, r, size) in enumerate(CHUNKS):
            if field == f:
                gathered[at][slot] = value[r:r + size]
        fixes[slot, 0, f] = jnp.where(eight == RIM - 1, faces[0] - 0.5 * regs[0], 0.0)
        fixes[slot, 1, f] = jnp.where(eight == 0, 0.5 * regs[1] - faces[1], 0.0)
        for at in range(columns // 128):
            lanes = slice(at * 128, at * 128 + 128)
            half = halves.at[slot, f, at]
            half[...] = value[:, lanes]
            averages[slot, f, :, lanes] = 0.5 * (half[pl.ds(0, CB, 2)] + half[pl.ds(1, CB, 2)])

    def refine_warmth(slot):
        old = around(slot, 2)
        below, above = shifted(old)
        edges = ghosts(old, transported(old, below, above, number))
        warmth = fine[slot, 2]
        regs = [0.0, 0.0]
        for left, right in edges:
            regs = [regs[0] + heat_flux(left, warmth[:1], number),
                    regs[1] + heat_flux(warmth[FB - 1:], right, number)]
            below, above = with_edges(warmth, left, right)
            warmth = transported(warmth, below, above, number)
        faces = [heat_flux(old[at - 1:at], old[at:at + 1], number) for at in (CB, 2 * CB)]
        keep_block(slot, 2, warmth, faces, regs)

    def refine_sound(slot):
        old_press, old_speed = around(slot, 0), around(slot, 1)
        new_press, new_speed, press_total, speed_total = acoustic_substeps(old_press, old_speed)
        press_edges, speed_edges = ghosts(old_press, new_press), ghosts(old_speed, new_speed)
        pressure, velocity = fine[slot, 0], fine[slot, 1]
        press_regs, speed_regs = [0.0, 0.0], [0.0, 0.0]
        for press_ends, speed_ends in zip(press_edges, speed_edges):
            press_sums, speed_sums = [4.0 * end for end in press_ends], [4.0 * end for end in speed_ends]
            for substep in range(4):
                press_sums = [press_sums[0] + pressure[:1], press_sums[1] + pressure[FB - 1:]]
                below, above = with_edges(pressure, *press_ends)
                velocity = velocity - HALF * (above - below)
                speed_sums = [speed_sums[0] + velocity[:1], speed_sums[1] + velocity[FB - 1:]]
                below, above = with_edges(velocity, *speed_ends)
                pressure = pressure - HALF * (above - below)
            press_regs = [reg + HALF * total for reg, total in zip(press_regs, press_sums)]
            speed_regs = [reg + HALF * total for reg, total in zip(speed_regs, speed_sums)]
        keep_block(slot, 0, pressure, face(speed_total), speed_regs)
        keep_block(slot, 1, velocity, face(press_total), press_regs)

    def each_pair(work):
        def two(at, carry):
            work(2 * at)
            work(2 * at + 1)
            return carry

        lax.fori_loop(0, FCAP // 2, two, 0)

    def bulk(load_from, store_to, skip):
        for first in range(0, columns, 128):
            lanes = slice(first, first + 128)
            span = pl.ds(load_from, ROWS_AT_ONCE + 2 * RIM)
            here = pl.ds(store_to, ROWS_AT_ONCE)
            keep = slice(skip, skip + ROWS_AT_ONCE)
            results = acoustic_substeps(coarse[0, span, lanes], coarse[1, span, lanes])
            out[0, here, lanes] = results[0][keep]
            out[1, here, lanes] = results[1][keep]
            warmth = coarse[2, span, lanes]
            below, above = shifted(warmth)
            out[2, here, lanes] = transported(warmth, below, above, number[:, lanes])[keep]

    pieces = rows // ROWS_AT_ONCE

    def bulk_some(low, high):
        def one(at, carry):
            start = pl.multiple_of(at * ROWS_AT_ONCE, ROWS_AT_ONCE)
            bulk(start - RIM, start, RIM)
            return carry

        lax.fori_loop(low, high, one, 0)

    def bulk_ends():
        bulk(0, 0, 0)
        bulk(rows - ROWS_AT_ONCE - 2 * RIM, rows - ROWS_AT_ONCE, 2 * RIM)

    def outer_rows():
        windows[0, :, RIM:] = coarse[:, :2 * RIM]
        windows[1, :, :2 * RIM] = coarse[:, rows - 2 * RIM:]
        for copy in rims:
            copy.wait()
        for side in range(2):
            keep = slice(RIM, 2 * RIM)
            put = slice(0, RIM) if side == 0 else slice(rows - RIM, rows)
            results = acoustic_substeps(windows[side, 0], windows[side, 1])
            out[0, put] = results[0][keep]
            out[1, put] = results[1][keep]
            warmth = windows[side, 2]
            below, above = shifted(warmth)
            out[2, put] = transported(warmth, below, above, number)[keep]

    def merge_fine():
        ranks = fine_count + PARENTS + 1

        def one(block, carry):
            before, here, after = [plan[ranks + block + at] for at in (-1, 0, 1)]
            low = pl.ds(pl.multiple_of(block * CB, CB), RIM)
            high = pl.ds(pl.multiple_of(block * CB + RIM, RIM), RIM)
            refined = jnp.full((RIM, columns), here, jnp.int32) < FCAP
            for f in range(3):
                mean = averages[here, f]
                out[f, low] = jnp.where(refined, mean[:RIM], out[f, low] + fixes[before, 1, f])
                out[f, high] = jnp.where(refined, mean[RIM:], out[f, high] + fixes[after, 0, f])
            return carry

        lax.fori_loop(0, B_DEV, one, 0)

    def held_at(code):
        owner = code // FCAP
        theirs = lax.rem(owner, QUAD)
        low = (theirs + spot) % 2
        high = (theirs // 2 + spot // 2) % 2
        return (2 * high + low) * FCAP + code - owner * FCAP

    def send_along(at):
        for step in list(range(1, line)) + [0]:
            for t in range(F_DEV):
                value = gathered[at][held_at(plan[others[step] * F_DEV + t])]
                if step:
                    leaving[at][step - 1, t] = value
                else:
                    landed[at][0, t] = value
            if step:
                along[at][step - 1].start()

    warm_parts = sum(f == 2 for f, r, size in CHUNKS)
    each_pair(refine_warmth)
    pl.semaphore_wait(barrier, len(greeted))
    for at in range(warm_parts):
        to_core[at].start()
        to_pair[at].start()
    each_pair(refine_sound)
    for copy in rims:
        copy.start()
    for at in range(warm_parts, parts):
        to_core[at].start()
    work = [lambda: bulk_some(1, 3), lambda: bulk_some(3, 5), lambda: bulk_some(5, pieces - 1),
            bulk_ends, outer_rows, merge_fine]
    for at in range(parts + 1):
        if at < parts:
            to_pair[at].wait_recv()
            passed[at].start()
            to_pair[at].wait_send()
            if at + warm_parts < parts:
                to_pair[at + warm_parts].start()
        if at >= 1:
            to_core[at - 1].wait_recv()
            passed[at - 1].wait_recv()
            send_along(at - 1)
            work[at - 1]()

    for at, (f, r, size) in enumerate(CHUNKS):
        for copy in along[at]:
            copy.wait_recv()
        for t in range(F_DEV):
            origin = plan[me * F_DEV + t] // (FCAP * QUAD)
            step = (place - origin + line) % line
            moved[t, f, r:r + size] = landed[at][step, t]
    for at in range(parts):
        for copy in [to_core[at], passed[at]] + along[at]:
            copy.wait_send()


def whole_step(devices, plan, courant, coarse, fine):
    columns = coarse.shape[2]
    line = devices // QUAD
    parts = len(CHUNKS)

    def per_chunk(*lead):
        return [pltpu.VMEM((*lead, size, columns), jnp.float32) for f, r, size in CHUNKS]

    dma = pltpu.SemaphoreType.DMA
    vmem = pl.BlockSpec(memory_space=pltpu.VMEM)
    return pl.pallas_call(
        functools.partial(step_kernel, devices),
        out_shape=(
            jax.ShapeDtypeStruct(coarse.shape, jnp.float32),
            jax.ShapeDtypeStruct((F_DEV, 3, FB, columns), jnp.float32),
        ),
        in_specs=[pl.BlockSpec(memory_space=pltpu.SMEM), vmem, vmem, vmem],
        out_specs=(vmem, vmem),
        scratch_shapes=[
            pltpu.VMEM((2, 3, 3 * RIM, columns), jnp.float32),
            pltpu.VMEM((B_DEV, 3, CB, columns), jnp.float32),
            pltpu.VMEM((FCAP + 1, 3, CB, columns), jnp.float32),
            pltpu.VMEM((FCAP + 1, 2, 3, RIM, columns), jnp.float32),
            pltpu.VMEM((FCAP, 3, columns // 128, FB, 128), jnp.float32),
            *per_chunk(QUAD * FCAP),
            *per_chunk(line - 1, F_DEV),
            *per_chunk(line, F_DEV),
            dma((parts,)), dma((parts,)), dma((parts,)), dma((parts,)), dma((parts,)), dma((parts,)),
            dma((parts * line,)), dma((parts * line,)), dma((4,)),
        ],
        compiler_params=pltpu.CompilerParams(
            collective_id=0, has_side_effects=True, vmem_limit_bytes=VMEM_LIMIT),
        name="whole_step",
    )(plan, courant[None, :], coarse, fine)


def per_device(devices, coarse, fine_old, refine_flags, new_slot, courant):
    plan = make_plan(refine_flags, new_slot)
    return whole_step(devices, plan, courant, coarse, fine_old)


def solution(mesh):
    placed = (
        P(None, ("group", "blk"), None),
        P(("group", "blk"), None, None, None),
        P("group"),
        P("group"),
        P("group"),
    )
    return jax.shard_map(
        functools.partial(per_device, mesh.shape["blk"]),
        mesh=mesh,
        in_specs=placed,
        out_specs=(P(None, ("group", "blk"), None), P(("group", "blk"), None, None, None)),
        check_vma=False,
    )
```

```python
import functools

import jax
import jax.numpy as jnp
from jax import lax
from jax.experimental import pallas as pl
from jax.experimental.pallas import tpu as pltpu
from jax.sharding import PartitionSpec as P

B_DEV = 32
CB = 16
FCAP = 6
FB = 32
F_DEV = 2
RIM = 8
QUAD = 4
ROWS_AT_ONCE = 64
PARENTS = 8
HALF = 0.3
MESH = pl.DeviceIdType.MESH
VMEM_LIMIT = 64 * 1024 * 1024
CHUNKS = ((2, 0, 16), (2, 16, 16), (0, 0, 16), (0, 16, 16), (1, 0, 16), (1, 16, 16))
AHEAD = 2


def shifted(field):
    count = field.shape[0]
    return pltpu.roll(field, 1, 0), pltpu.roll(field, count - 1, 0)


def acoustic_substeps(pressure, velocity):
    press_sum = speed_sum = 0.0
    for substep in range(4):
        press_sum = press_sum + pressure
        below, above = shifted(pressure)
        velocity = velocity - HALF * (above - below)
        speed_sum = speed_sum + velocity
        below, above = shifted(velocity)
        pressure = pressure - HALF * (above - below)
    return pressure, velocity, press_sum, speed_sum


def heat_flux(low, high, courant):
    return 0.5 * courant * (low + high) - 0.5 * courant * courant * (high - low)


def transported(warmth, below, above, courant):
    return warmth - (heat_flux(warmth, above, courant) - heat_flux(below, warmth, courant))


def plan_kernel(flags_at, slots_at, plan, flags, slots, sems):
    get_flags = pltpu.make_async_copy(flags_at, flags, sems.at[0])
    get_slots = pltpu.make_async_copy(slots_at, slots, sems.at[1])
    get_flags.start()
    get_slots.start()
    get_flags.wait()
    get_slots.wait()
    me = lax.axis_index("blk")
    owners = flags.shape[0] // B_DEV
    fine_count = slots.shape[0]

    def list_owner(owner, base):
        total = flags[owner * B_DEV]
        for at in range(1, B_DEV):
            total = total + flags[owner * B_DEV + at]

        def list_block(rank, carry):
            plan[slots[base + rank]] = owner * FCAP + rank
            return carry

        lax.fori_loop(0, total, list_block, 0)
        return base + total

    lax.fori_loop(0, owners, list_owner, 0)
    for slot in range(PARENTS):
        plan[fine_count + slot] = 0
    ranks = fine_count + PARENTS + 1
    plan[ranks - 1] = FCAP
    plan[ranks + B_DEV] = FCAP
    count = jnp.int32(0)
    for block in range(1, B_DEV - 1):
        flag = flags[me * B_DEV + block]
        before = plan[fine_count + count]
        plan[fine_count + count] = jnp.where(flag == 1, block - 1, before)
        plan[ranks + block] = jnp.where(flag == 1, count, FCAP)
        count = count + flag
    plan[ranks] = FCAP
    plan[ranks + B_DEV - 1] = FCAP


def make_plan(flags, slots):
    return pl.pallas_call(
        plan_kernel,
        out_shape=jax.ShapeDtypeStruct((slots.shape[0] + PARENTS + B_DEV + 2,), jnp.int32),
        in_specs=[pl.BlockSpec(memory_space=pltpu.HBM)] * 2,
        out_specs=pl.BlockSpec(memory_space=pltpu.SMEM),
        scratch_shapes=[
            pltpu.SMEM(flags.shape, jnp.int32),
            pltpu.SMEM(slots.shape, jnp.int32),
            pltpu.SemaphoreType.DMA((2,)),
        ],
        name="make_plan",
    )(flags, slots)


def step_kernel(devices, plan, courant_at, coarse_at, blocks_at, fine_at, out, moved,
                courant, coarse, press_blocks, speed_blocks, warm_blocks, fine, fetch_sems,
                windows, averages, fixes, halves, *scratch):
    parts = len(CHUNKS)
    gathered, leaving, landed = scratch[:parts], scratch[parts:2 * parts], scratch[2 * parts:3 * parts]
    core_send, core_recv, pair_send, pair_recv, pass_send, pass_recv, line_send, line_recv, rim_sems = scratch[3 * parts:]
    rows, columns = coarse.shape[1], coarse.shape[2]
    fine_count = devices * F_DEV
    line = devices // QUAD
    group = lax.axis_index("group")
    me = lax.axis_index("blk")
    spot = lax.rem(me, QUAD)
    place = me // QUAD
    core = me + 1 - 2 * lax.rem(me, 2)
    pair = me + 2 - 4 * (spot // 2)
    up = lax.rem(me + 1, devices)
    down = lax.rem(me + devices - 1, devices)
    others = [lax.rem(me + QUAD * step, devices) for step in range(line)]

    barrier = pltpu.get_barrier_semaphore()
    greeted = [core, pair, up, down] + others[1:]
    for other in greeted:
        pl.semaphore_signal(barrier, inc=1, device_id=(group, other), device_id_type=MESH)

    averages[FCAP] = jnp.zeros(averages.shape[1:], jnp.float32)
    fixes[FCAP] = jnp.zeros(fixes.shape[1:], jnp.float32)

    blocks = (press_blocks, speed_blocks, warm_blocks)
    fetched = [
        pltpu.make_async_copy(source, target, fetch_sems.at[at])
        for at, (source, target) in enumerate([
            (courant_at, courant), (blocks_at.at[2], warm_blocks),
            (fine_at.at[:, pl.ds(2, 1)], fine.at[:, pl.ds(2, 1)]),
            (blocks_at.at[0], press_blocks), (blocks_at.at[1], speed_blocks),
            (fine_at.at[:, pl.ds(0, 2)], fine.at[:, pl.ds(0, 2)]), (coarse_at, coarse)])]
    for copy in fetched:
        copy.start()

    def remote(source, target, send, recv, device):
        return pltpu.make_async_remote_copy(
            src_ref=source, dst_ref=target, send_sem=send, recv_sem=recv,
            device_id=(group, device), device_id_type=MESH)

    own, from_core, from_pair, from_far = [pl.ds(FCAP * at, FCAP) for at in range(QUAD)]
    to_pair, to_core, passed, along = [], [], [], []
    for at in range(parts):
        buffer = gathered[at]
        to_pair.append(remote(buffer.at[own], buffer.at[from_pair], pair_send.at[at], pair_recv.at[at], pair))
        to_core.append(remote(buffer.at[own], buffer.at[from_core], core_send.at[at], core_recv.at[at], core))
        passed.append(remote(buffer.at[from_pair], buffer.at[from_far], pass_send.at[at], pass_recv.at[at], core))
        along.append([
            remote(leaving[at].at[step - 1], landed[at].at[step],
                   line_send.at[at * line + step], line_recv.at[at * line + step], others[step])
            for step in range(1, line)])
    rims = [
        remote(coarse_at.at[:, pl.ds(0, RIM)], windows.at[1, :, pl.ds(2 * RIM, RIM)], rim_sems.at[0], rim_sems.at[1], down),
        remote(coarse_at.at[:, pl.ds(rows - RIM, RIM)], windows.at[0, :, pl.ds(0, RIM)], rim_sems.at[2], rim_sems.at[3], up),
    ]

    for copy in fetched[:3]:
        copy.wait()
    number = courant[...]
    row_at = lax.broadcasted_iota(jnp.int32, (FB, columns), 0)
    eight = lax.broadcasted_iota(jnp.int32, (RIM, columns), 0)

    def with_edges(field, left, right):
        below, above = shifted(field)
        return (jnp.where(row_at == 0, left, below), jnp.where(row_at == FB - 1, right, above))

    def around(slot, f):
        block = plan[fine_count + slot]
        return jnp.concatenate([blocks[f][block], blocks[f][block + 1], blocks[f][block + 2]], 0)

    def ghosts(old, new):
        pairs = [(old[CB - 1:CB], new[CB - 1:CB]), (old[2 * CB:2 * CB + 1], new[2 * CB:2 * CB + 1])]
        return [[o + 0.5 * fine_round * (n - o) for o, n in pairs] for fine_round in range(2)]

    def face(total):
        return [HALF * (total[CB - 1:CB] + total[CB:CB + 1]),
                HALF * (total[2 * CB - 1:2 * CB] + total[2 * CB:2 * CB + 1])]

    def keep_block(slot, f, value, faces, regs):
        for at, (field, r, size) in enumerate(CHUNKS):
            if field == f:
                gathered[at][slot] = value[r:r + size]
        fixes[slot, 0, f] = jnp.where(eight == RIM - 1, faces[0] - 0.5 * regs[0], 0.0)
        fixes[slot, 1, f] = jnp.where(eight == 0, 0.5 * regs[1] - faces[1], 0.0)
        for at in range(columns // 128):
            lanes = slice(at * 128, at * 128 + 128)
            half = halves.at[slot, f, at]
            half[...] = value[:, lanes]
            averages[slot, f, :, lanes] = 0.5 * (half[pl.ds(0, CB, 2)] + half[pl.ds(1, CB, 2)])

    def refine_warmth(slot):
        old = around(slot, 2)
        below, above = shifted(old)
        edges = ghosts(old, transported(old, below, above, number))
        warmth = fine[slot, 2]
        regs = [0.0, 0.0]
        for left, right in edges:
            regs = [regs[0] + heat_flux(left, warmth[:1], number),
                    regs[1] + heat_flux(warmth[FB - 1:], right, number)]
            below, above = with_edges(warmth, left, right)
            warmth = transported(warmth, below, above, number)
        faces = [heat_flux(old[at - 1:at], old[at:at + 1], number) for at in (CB, 2 * CB)]
        keep_block(slot, 2, warmth, faces, regs)

    def refine_sound(slot):
        old_press, old_speed = around(slot, 0), around(slot, 1)
        new_press, new_speed, press_total, speed_total = acoustic_substeps(old_press, old_speed)
        press_edges, speed_edges = ghosts(old_press, new_press), ghosts(old_speed, new_speed)
        pressure, velocity = fine[slot, 0], fine[slot, 1]
        press_regs, speed_regs = [0.0, 0.0], [0.0, 0.0]
        for press_ends, speed_ends in zip(press_edges, speed_edges):
            press_sums, speed_sums = [4.0 * end for end in press_ends], [4.0 * end for end in speed_ends]
            for substep in range(4):
                press_sums = [press_sums[0] + pressure[:1], press_sums[1] + pressure[FB - 1:]]
                below, above = with_edges(pressure, *press_ends)
                velocity = velocity - HALF * (above - below)
                speed_sums = [speed_sums[0] + velocity[:1], speed_sums[1] + velocity[FB - 1:]]
                below, above = with_edges(velocity, *speed_ends)
                pressure = pressure - HALF * (above - below)
            press_regs = [reg + HALF * total for reg, total in zip(press_regs, press_sums)]
            speed_regs = [reg + HALF * total for reg, total in zip(speed_regs, speed_sums)]
        keep_block(slot, 0, pressure, face(speed_total), speed_regs)
        keep_block(slot, 1, velocity, face(press_total), press_regs)

    def each_pair(work):
        def two(at, carry):
            work(2 * at)
            work(2 * at + 1)
            return carry

        lax.fori_loop(0, FCAP // 2, two, 0)

    def bulk(load_from, store_to, skip):
        for first in range(0, columns, 128):
            lanes = slice(first, first + 128)
            span = pl.ds(load_from, ROWS_AT_ONCE + 2 * RIM)
            here = pl.ds(store_to, ROWS_AT_ONCE)
            keep = slice(skip, skip + ROWS_AT_ONCE)
            results = acoustic_substeps(coarse[0, span, lanes], coarse[1, span, lanes])
            out[0, here, lanes] = results[0][keep]
            out[1, here, lanes] = results[1][keep]
            warmth = coarse[2, span, lanes]
            below, above = shifted(warmth)
            out[2, here, lanes] = transported(warmth, below, above, number[:, lanes])[keep]

    pieces = rows // ROWS_AT_ONCE

    def bulk_some(low, high):
        def one(at, carry):
            start = pl.multiple_of(at * ROWS_AT_ONCE, ROWS_AT_ONCE)
            bulk(start - RIM, start, RIM)
            return carry

        lax.fori_loop(low, high, one, 0)

    def bulk_ends():
        bulk(0, 0, 0)
        bulk(rows - ROWS_AT_ONCE - 2 * RIM, rows - ROWS_AT_ONCE, 2 * RIM)

    def outer_rows():
        windows[0, :, RIM:] = coarse[:, :2 * RIM]
        windows[1, :, :2 * RIM] = coarse[:, rows - 2 * RIM:]
        for copy in rims:
            copy.wait()
        for side in range(2):
            keep = slice(RIM, 2 * RIM)
            put = slice(0, RIM) if side == 0 else slice(rows - RIM, rows)
            results = acoustic_substeps(windows[side, 0], windows[side, 1])
            out[0, put] = results[0][keep]
            out[1, put] = results[1][keep]
            warmth = windows[side, 2]
            below, above = shifted(warmth)
            out[2, put] = transported(warmth, below, above, number)[keep]

    def merge_fine():
        ranks = fine_count + PARENTS + 1

        def one(block, carry):
            before, here, after = [plan[ranks + block + at] for at in (-1, 0, 1)]
            low = pl.ds(pl.multiple_of(block * CB, CB), RIM)
            high = pl.ds(pl.multiple_of(block * CB + RIM, RIM), RIM)
            refined = jnp.full((RIM, columns), here, jnp.int32) < FCAP
            for f in range(3):
                mean = averages[here, f]
                out[f, low] = jnp.where(refined, mean[:RIM], out[f, low] + fixes[before, 1, f])
                out[f, high] = jnp.where(refined, mean[RIM:], out[f, high] + fixes[after, 0, f])
            return carry

        lax.fori_loop(0, B_DEV, one, 0)

    def held_at(code):
        owner = code // FCAP
        theirs = lax.rem(owner, QUAD)
        low = (theirs + spot) % 2
        high = (theirs // 2 + spot // 2) % 2
        return (2 * high + low) * FCAP + code - owner * FCAP

    def send_along(at):
        for step in list(range(1, line)) + [0]:
            for t in range(F_DEV):
                value = gathered[at][held_at(plan[others[step] * F_DEV + t])]
                if step:
                    leaving[at][step - 1, t] = value
                else:
                    landed[at][0, t] = value
            if step:
                along[at][step - 1].start()

    warm_parts = sum(f == 2 for f, r, size in CHUNKS)
    each_pair(refine_warmth)
    pl.semaphore_wait(barrier, len(greeted))
    for at in range(warm_parts):
        to_core[at].start()
        if at < AHEAD:
            to_pair[at].start()
    for copy in fetched[3:]:
        copy.wait()
    each_pair(refine_sound)
    for copy in rims:
        copy.start()
    for at in range(warm_parts, parts):
        to_core[at].start()
    work = [lambda: bulk_some(1, 3), lambda: bulk_some(3, 5), lambda: bulk_some(5, pieces - 1),
            bulk_ends, outer_rows, merge_fine]
    for at in range(parts + 1):
        if at < parts:
            to_pair[at].wait_recv()
            passed[at].start()
            to_pair[at].wait_send()
            if at + AHEAD < parts:
                to_pair[at + AHEAD].start()
        if at >= 1:
            to_core[at - 1].wait_recv()
            passed[at - 1].wait_recv()
            send_along(at - 1)
            for piece in work[(at - 1) * len(work) // parts:at * len(work) // parts]:
                piece()

    for at, (f, r, size) in enumerate(CHUNKS):
        for copy in along[at]:
            copy.wait_recv()
        for t in range(F_DEV):
            origin = plan[me * F_DEV + t] // (FCAP * QUAD)
            step = (place - origin + line) % line
            moved[t, f, r:r + size] = landed[at][step, t]
    for at in range(parts):
        for copy in [to_core[at], passed[at]] + along[at]:
            copy.wait_send()


def whole_step(devices, plan, courant, coarse, fine):
    columns = coarse.shape[2]
    line = devices // QUAD
    parts = len(CHUNKS)

    def per_chunk(*lead):
        return [pltpu.VMEM((*lead, size, columns), jnp.float32) for f, r, size in CHUNKS]

    dma = pltpu.SemaphoreType.DMA
    vmem = pl.BlockSpec(memory_space=pltpu.VMEM)
    return pl.pallas_call(
        functools.partial(step_kernel, devices),
        out_shape=(
            jax.ShapeDtypeStruct(coarse.shape, jnp.float32),
            jax.ShapeDtypeStruct((F_DEV, 3, FB, columns), jnp.float32),
        ),
        in_specs=[pl.BlockSpec(memory_space=pltpu.SMEM)] + [pl.BlockSpec(memory_space=pltpu.HBM)] * 4,
        out_specs=(vmem, vmem),
        scratch_shapes=[
            pltpu.VMEM((1, columns), jnp.float32),
            pltpu.VMEM(coarse.shape, jnp.float32),
            *[pltpu.VMEM((B_DEV, CB, columns), jnp.float32)] * 3,
            pltpu.VMEM(fine.shape, jnp.float32),
            dma((7,)),
            pltpu.VMEM((2, 3, 3 * RIM, columns), jnp.float32),
            pltpu.VMEM((FCAP + 1, 3, CB, columns), jnp.float32),
            pltpu.VMEM((FCAP + 1, 2, 3, RIM, columns), jnp.float32),
            pltpu.VMEM((FCAP, 3, columns // 128, FB, 128), jnp.float32),
            *per_chunk(QUAD * FCAP),
            *per_chunk(line - 1, F_DEV),
            *per_chunk(line, F_DEV),
            dma((parts,)), dma((parts,)), dma((parts,)), dma((parts,)), dma((parts,)), dma((parts,)),
            dma((parts * line,)), dma((parts * line,)), dma((4,)),
        ],
        compiler_params=pltpu.CompilerParams(
            collective_id=0, has_side_effects=True, vmem_limit_bytes=VMEM_LIMIT),
        name="whole_step",
    )(plan, courant[None, :], coarse, coarse.reshape(3, B_DEV, CB, columns), fine)


def place_kernel(coarse_at, fine_at, coarse_to, fine_to, coarse, fine, in_sems, out_sems):
    half = coarse.shape[1] // 2
    views = [(fine_at, fine, fine_to)]
    for f in range(3):
        for first in (0, half):
            views.append([ref.at[f, pl.ds(first, half)] for ref in (coarse_at, coarse, coarse_to)])
    inward = [pltpu.make_async_copy(source, held, in_sems.at[at])
              for at, (source, held, target) in enumerate(views)]
    outward = [pltpu.make_async_copy(held, target, out_sems.at[at])
               for at, (source, held, target) in enumerate(views)]
    for copy in inward:
        copy.start()
    for come, go in zip(inward, outward):
        come.wait()
        go.start()
    for copy in outward:
        copy.wait()


def place(coarse, fine):
    hbm = pl.BlockSpec(memory_space=pltpu.HBM)
    return pl.pallas_call(
        place_kernel,
        out_shape=tuple(jax.ShapeDtypeStruct(x.shape, x.dtype) for x in (coarse, fine)),
        in_specs=[hbm, hbm],
        out_specs=(hbm, hbm),
        scratch_shapes=[
            pltpu.VMEM(coarse.shape, jnp.float32),
            pltpu.VMEM(fine.shape, jnp.float32),
            pltpu.SemaphoreType.DMA((7,)),
            pltpu.SemaphoreType.DMA((7,)),
        ],
        compiler_params=pltpu.CompilerParams(vmem_limit_bytes=VMEM_LIMIT),
        name="place",
    )(coarse, fine)


def per_device(devices, coarse, fine_old, refine_flags, new_slot, courant):
    plan = make_plan(refine_flags, new_slot)
    return place(*whole_step(devices, plan, courant, coarse, fine_old))


def solution(mesh):
    placed = (
        P(None, ("group", "blk"), None),
        P(("group", "blk"), None, None, None),
        P("group"),
        P("group"),
        P("group"),
    )
    return jax.shard_map(
        functools.partial(per_device, mesh.shape["blk"]),
        mesh=mesh,
        in_specs=placed,
        out_specs=(P(None, ("group", "blk"), None), P(("group", "blk"), None, None, None)),
        check_vma=False,
    )
```
